256 devices in a mesh: dp: 8 (over x, core), ctx: 32 (over y, z).
Axes of the slice: x: 4, y: 4, z: 8, core: 2. Of those that a mesh axis runs over, the one named last changes fastest.
Arguments:
- queries: bfloat16 [32768, 4096], P(('dp', 'ctx')), may hold values from -128 to 128
- keys: bfloat16 [32768, 512], P(('dp', 'ctx')), may hold values from -8 to 8
- values: bfloat16 [32768, 512], P(('dp', 'ctx')), may hold values from -6 to 6
- output_gradient: bfloat16 [32768, 4096], P(('dp', 'ctx')), may hold values from -6 to 6
- doc_lengths: int32 [8, 3], replicated, may hold values from 1 to 4, 8 in all within a row
- dest_group: int32 [64], replicated, may hold values from 0 to 7, as said below
- dest_slot: int32 [64], replicated, may hold values from 0 to 7, as said below
Outputs:
- grad_q: bfloat16 [32768, 4096], P(('dp', 'ctx'))
- key_gradient: bfloat16 [32768, 512], P(('dp', 'ctx'))
- value_gradient: bfloat16 [32768, 512], P(('dp', 'ctx'))
The draws below stay inside these ranges and needn't reach their ends.
Inputs may be any that keep to these rules, and one draw needn't show every extreme that they name: `dest_group`: every group receives exactly 8 blocks, and each group sends to each group either none or exactly 2 of its blocks. The pair of dest_group and dest_slot differs for every block, so every slot of every group is filled once. `doc_lengths`: each row sums to 8; its longest document has exactly 4 blocks.
All inputs are finite; a program needn't handle non-finite values.
Results may differ from the reference program's by a relative error of at most 0.035.
Values may be sent and summed in bfloat16 or wider, within the bound.
No kernel may reach another device: no remote copies, remote signals or barrier semaphores. Data moves between devices by JAX's collectives and lax.ppermute only.
A program may use at most 128 MiB of HBM per device.

```python
import math
import jax
import jax.numpy as jnp
import numpy as np
from jax import lax

QUERY_HEADS = 32
KEY_HEADS = 4
HEAD_SIZE = 128
BLOCK = 512
GROUP_BLOCKS = 8
NDOC = 3
QUERIES_PER_KEY = 8
CAP = 2
BR = 16
TOK_DEV = 128
GROUP_TOKENS = 4096
TOTAL_TOKENS = 32768
N_DP = 8
N_CTX = 32


def shared_base(key):
    return jax.random.normal(key, (TOTAL_TOKENS, KEY_HEADS * HEAD_SIZE), jnp.float32)


def draw_keys(key, part):
    base_offset = shared_base(key)
    result = base_offset
    return result.astype(jnp.bfloat16)


def draw_queries(key, part):
    key = jax.random.fold_in(key, 23)
    result = jax.random.normal(key, (TOTAL_TOKENS, QUERY_HEADS * HEAD_SIZE), jnp.float32)
    return result.astype(jnp.bfloat16)


def routing(key):
    first, second, third, fourth = jax.random.split(key, 4)
    relabel = jax.random.permutation(first, N_DP)
    offsets = jax.random.permutation(second, N_DP)[:GROUP_BLOCKS // CAP]
    order = jax.random.permutation(third, GROUP_BLOCKS)
    shifted = offsets[order // CAP]
    groups = jnp.arange(N_DP)
    target = relabel[(groups[:, None] + shifted[None, :]) % N_DP]
    tables = jax.vmap(lambda sub: jax.random.permutation(sub, GROUP_BLOCKS))(jax.random.split(fourth, N_DP))
    placed = tables[target, jnp.arange(GROUP_BLOCKS)[None, :]]
    return (target.reshape(-1), placed.reshape(-1))


def draw_dest_group(key, part):
    target, placed = routing(key)
    return target.astype(jnp.int32)


def draw_dest_slot(key, part):
    target, placed = routing(key)
    return placed.astype(jnp.int32)


def block_scale(key, dims, cuts, smallest, top_value):
    gain, own = 1.0, jax.random.fold_in(key, 6)
    for position, parts in cuts:
        steps = jnp.exp(jax.random.uniform(jax.random.fold_in(own, position), (parts,), jnp.float32, smallest / len(cuts), top_value / len(cuts)))
        gain = gain * jnp.repeat(steps, dims[position] // parts).reshape([-1 if axis == position else 1 for axis in range(len(dims))])
    return gain


def length_profile(amount, total, limit, skew):
    loads = [(1 << 20) // math.isqrt(rank ** skew) + 1 for rank in range(2, amount + 1)]
    spare, given = total - limit - (amount - 1), [1] * (amount - 1)
    while spare > 0:
        candidates = [i for i in range(amount - 1) if given[i] < limit]
        whole, left = sum([loads[i] for i in candidates]), spare
        for i in candidates:
            addition = min(limit - given[i], max(1, left * loads[i] // whole), spare)
            given[i] = given[i] + addition
            spare = spare - addition
    return np.array([limit] + given)


def uneven(own_key, number_of, total, most, slope):
    if number_of == 2:
        one = jax.random.randint(own_key, (), max(1, total - most), min(most, total - 1) + 1)
        return jnp.stack([one, total - one])
    lengths = jnp.asarray(length_profile(number_of, total, most, slope), jnp.int32)
    couples = (number_of - 1) // 2
    giver, receiver = lengths[1:1 + 2 * couples:2], lengths[2:2 + 2 * couples:2]
    room = jnp.minimum(giver - 1, most - receiver)
    passed = jax.random.randint(jax.random.fold_in(own_key, 1), (couples,), 0, 1 << 20) % (room + 1)
    lengths = lengths.at[1:1 + 2 * couples:2].set(giver - passed).at[2:2 + 2 * couples:2].set(receiver + passed)
    return lengths[jax.random.permutation(jax.random.fold_in(own_key, 2), number_of)]


def normal_values(own_key, extent, scale, most, cuts=(), kind=jnp.bfloat16):
    gain = block_scale(own_key, extent, cuts, -0.22, 0.18) if cuts else 1.0
    values = jax.random.normal(own_key, extent, jnp.float32) * scale * gain
    return jnp.minimum(jnp.maximum(values, -most), most).astype(kind)


def setup_inputs(seed: int = 0) -> dict:
    streams_of = jax.random.split(jax.random.key(seed), 8)
    queries = draw_queries(jax.random.fold_in(streams_of[7], 71), 0)
    keys = draw_keys(jax.random.fold_in(streams_of[7], 71), 0)
    values = normal_values(streams_of[2], (TOTAL_TOKENS, KEY_HEADS * HEAD_SIZE), 1.0, 6.0, ((0, 256),))
    output_gradient = normal_values(streams_of[3], (TOTAL_TOKENS, QUERY_HEADS * HEAD_SIZE), 1.0, 6.0, ((0, 256),))
    doc_lengths = jax.vmap(lambda own: uneven(own, NDOC, GROUP_BLOCKS, GROUP_BLOCKS // 2, 2))(jax.random.split(streams_of[4], N_DP)).reshape((N_DP, NDOC)).astype(jnp.int32)
    dest_group = draw_dest_group(jax.random.fold_in(streams_of[7], 71), 0)
    dest_slot = draw_dest_slot(jax.random.fold_in(streams_of[7], 71), 0)
    return {"queries": queries, "keys": keys, "values": values, "output_gradient": output_gradient, "doc_lengths": doc_lengths, "dest_group": dest_group, "dest_slot": dest_slot}


NEG = -1.0e30


def reference(queries, keys, values, output_gradient, doc_lengths, dest_group, dest_slot):
    score_scale = HEAD_SIZE ** -0.5
    hp = lax.Precision.HIGHEST
    blocks_all = jnp.arange(N_DP * GROUP_BLOCKS, dtype=jnp.int32)
    groups = jnp.arange(N_DP, dtype=jnp.int32)
    slots = jnp.arange(GROUP_BLOCKS, dtype=jnp.int32)
    hit = (dest_group[None, None, :] == groups[:, None, None]) & (dest_slot[None, None, :] == slots[None, :, None])
    source = jnp.sum(jnp.where(hit, blocks_all[None, None, :], 0), axis=2).astype(jnp.int32)
    anchor_group = source // GROUP_BLOCKS
    anchor_block = source % GROUP_BLOCKS
    columns = jnp.arange(N_CTX, dtype=jnp.int32)
    within = jnp.arange(BR, dtype=jnp.int32)
    index = (anchor_group[:, :, None, None] * N_CTX + columns[None, None, :, None]) * TOK_DEV
    index = index + anchor_block[:, :, None, None] * BR + within[None, None, None, :]
    index = index.reshape(N_DP, GROUP_TOKENS).astype(jnp.int32)
    ends = jnp.cumsum(doc_lengths, axis=1)
    segment = jnp.sum((ends[:, None, :] <= slots[None, :, None]).astype(jnp.int32), axis=2).astype(jnp.int32)
    window = GROUP_BLOCKS // 2

    def one_group(inputs):
        token_rows, seg = inputs
        query_input = queries[token_rows].reshape(GROUP_TOKENS, KEY_HEADS, QUERIES_PER_KEY, HEAD_SIZE)
        upstream_gradient = output_gradient[token_rows].reshape(GROUP_TOKENS, KEY_HEADS, QUERIES_PER_KEY, HEAD_SIZE)
        key = keys[token_rows].reshape(GROUP_TOKENS, KEY_HEADS, HEAD_SIZE)
        value_input = values[token_rows].reshape(GROUP_TOKENS, KEY_HEADS, HEAD_SIZE)
        token_seg = jnp.repeat(seg, BLOCK)
        positions = jnp.arange(GROUP_TOKENS, dtype=jnp.int32)

        def per_slot(carry, slot):
            key_gradient_rows, value_gradient_rows = carry
            start = (jnp.clip(slot - window + 1, 0, GROUP_BLOCKS - window) * BLOCK).astype(jnp.int32)
            first = (slot * BLOCK).astype(jnp.int32)
            qs = lax.dynamic_slice_in_dim(query_input, first, BLOCK, 0).astype(jnp.float32)
            gs = lax.dynamic_slice_in_dim(upstream_gradient, first, BLOCK, 0).astype(jnp.float32)
            ks = lax.dynamic_slice_in_dim(key, start, window * BLOCK, 0).astype(jnp.float32)
            vs = lax.dynamic_slice_in_dim(value_input, start, window * BLOCK, 0).astype(jnp.float32)
            q_pos = lax.dynamic_slice_in_dim(positions, first, BLOCK, 0)
            k_pos = lax.dynamic_slice_in_dim(positions, start, window * BLOCK, 0)
            q_seg = lax.dynamic_slice_in_dim(token_seg, first, BLOCK, 0)
            k_seg = lax.dynamic_slice_in_dim(token_seg, start, window * BLOCK, 0)
            visible = (k_seg[None, :] == q_seg[:, None]) & (k_pos[None, :] <= q_pos[:, None])
            score = jnp.einsum("qhgd,khd->hgqk", qs, ks, precision=hp) * score_scale
            score = jnp.where(visible[None, None], score, NEG)
            top = jnp.max(score, axis=-1, keepdims=True)
            raw = jnp.where(visible[None, None], jnp.exp(score - top), 0.0)
            prob = raw / jnp.sum(raw, axis=-1, keepdims=True)
            rounded = lax.optimization_barrier(prob.astype(jnp.bfloat16)).astype(jnp.float32)
            attended = jnp.einsum("hgqk,khd->qhgd", rounded, vs, precision=hp).astype(jnp.bfloat16)
            attended = lax.optimization_barrier(attended).astype(jnp.float32)
            delta = jnp.sum(gs * attended, axis=-1)
            dprob = jnp.einsum("qhgd,khd->hgqk", gs, vs, precision=hp)
            dscore = prob * (dprob - jnp.transpose(delta, (1, 2, 0))[..., None])
            dscore = lax.optimization_barrier(dscore.astype(jnp.bfloat16)).astype(jnp.float32)
            grad_query = (score_scale * jnp.einsum("hgqk,khd->qhgd", dscore, ks, precision=hp)).astype(jnp.bfloat16)
            key_term = jnp.einsum("hgqk,qhgd->khd", dscore, qs, precision=hp)
            val_term = jnp.einsum("hgqk,qhgd->khd", rounded, gs, precision=hp)
            key_gradient_rows = lax.dynamic_update_slice_in_dim(
                key_gradient_rows, lax.dynamic_slice_in_dim(key_gradient_rows, start, window * BLOCK, 0) + key_term, start, 0)
            value_gradient_rows = lax.dynamic_update_slice_in_dim(
                value_gradient_rows, lax.dynamic_slice_in_dim(value_gradient_rows, start, window * BLOCK, 0) + val_term, start, 0)
            return (key_gradient_rows, value_gradient_rows), grad_query

        zero_fill = jnp.zeros((GROUP_TOKENS, KEY_HEADS, HEAD_SIZE), jnp.float32)
        (key_gradient_rows, value_gradient_rows), grad_query = lax.scan(per_slot, (zero_fill, zero_fill), jnp.arange(GROUP_BLOCKS, dtype=jnp.int32))
        return (grad_query.reshape(GROUP_TOKENS, QUERY_HEADS * HEAD_SIZE),
                (score_scale * key_gradient_rows).astype(jnp.bfloat16).reshape(GROUP_TOKENS, KEY_HEADS * HEAD_SIZE),
                value_gradient_rows.astype(jnp.bfloat16).reshape(GROUP_TOKENS, KEY_HEADS * HEAD_SIZE))

    grad_query, key_gradient_rows, value_gradient_rows = lax.map(one_group, (index, segment))
    flat_rows = index.reshape(-1)
    out_q = jnp.zeros((TOTAL_TOKENS, QUERY_HEADS * HEAD_SIZE), jnp.bfloat16).at[flat_rows].set(grad_query.reshape(-1, QUERY_HEADS * HEAD_SIZE))
    output_keys = jnp.zeros((TOTAL_TOKENS, KEY_HEADS * HEAD_SIZE), jnp.bfloat16).at[flat_rows].set(key_gradient_rows.reshape(-1, KEY_HEADS * HEAD_SIZE))
    output_values = jnp.zeros((TOTAL_TOKENS, KEY_HEADS * HEAD_SIZE), jnp.bfloat16).at[flat_rows].set(value_gradient_rows.reshape(-1, KEY_HEADS * HEAD_SIZE))
    return (out_q, output_keys, output_values)
```

```python
import math

import jax
import jax.numpy as jnp
from jax import lax
from jax.experimental import pallas as pl
from jax.experimental.pallas import tpu as pltpu
from jax.sharding import Mesh, PartitionSpec as P

QUERY_HEADS = 32
KEY_HEADS = 4
HEAD = 128
SLOTS = 8
BLOCK = 512
PER_KEY = QUERY_HEADS // KEY_HEADS
WIDE = PER_KEY * HEAD
BR = 16
CAP = 2
N_DP = 8
N_Y = 4
N_Z = 8
HALF = BLOCK // 2
SPAN = SLOTS // 2
NEG = -1.0e30
SCALE = HEAD ** -0.5
EXP_SCALE = SCALE / math.log(2.0)
F32 = jnp.float32
BF16 = jnp.bfloat16
MIB = 1024 * 1024


def tables(doc_lengths, dest_group, dest_slot):
    me = lax.axis_index("dp")
    blocks = jnp.arange(SLOTS, dtype=jnp.int32)
    dest = dest_group.reshape(N_DP, SLOTS)
    slot = dest_slot.reshape(N_DP, SLOTS)
    earlier = (dest[:, :, None] == dest[:, None, :]) & (blocks[None, :] < blocks[:, None])[None]
    rank = jnp.sum(earlier.astype(jnp.int32), axis=2)
    mine = blocks == me
    hit = ((dest == me)[None] & (slot[None] == blocks[:, None, None])).astype(jnp.int32)
    from_group = jnp.sum(hit * blocks[None, :, None], axis=(1, 2))
    from_rank = jnp.sum(hit * rank[None], axis=(1, 2))
    lengths = jnp.sum(jnp.where(mine[:, None], doc_lengths, 0), axis=0)
    docs = jnp.arange(lengths.shape[0], dtype=jnp.int32)
    ends = jnp.sum(jnp.where(docs[None, :] <= docs[:, None], lengths[None, :], 0), axis=1)
    first = jnp.max(jnp.where(ends[None, :] <= blocks[:, None], ends[None, :], 0), axis=1)
    place = jnp.full((SLOTS,), lax.axis_index("z"), jnp.int32)
    return jnp.stack([from_group, from_rank, first, place]).astype(jnp.int32)


def params(mib):
    return pltpu.CompilerParams(vmem_limit_bytes=mib * MIB)


def to_source(s, t):
    return (t[0, s], 0, t[1, s], 0, 0)


def whole(space):
    return pl.BlockSpec(memory_space=space)


def route(dest):
    base = lax.axis_index("dp") * SLOTS
    groups = [dest[base + j] for j in range(SLOTS)]
    ranks = []
    for j in range(SLOTS):
        rank = jnp.int32(0)
        for i in range(j):
            rank = rank + jnp.where(groups[i] == groups[j], 1, 0).astype(jnp.int32)
        ranks.append(rank)
    return list(zip(groups, ranks))


def run(copies):
    for copy in copies:
        copy.start()
    for copy in copies:
        copy.wait()


def pack_pair_body(dest, k, v, out, stage, sem):
    copies = []
    for j, (group, rank) in enumerate(route(dest)):
        rows = slice(j * BR, (j + 1) * BR)
        for h in range(KEY_HEADS):
            cols = slice(h * HEAD, (h + 1) * HEAD)
            stage[j, h, :, :HEAD] = k[rows, cols]
            stage[j, h, :, HEAD:] = v[rows, cols]
        copies.append(pltpu.make_async_copy(stage.at[j], out.at[group, :, rank], sem.at[j]))
    run(copies)


def pack_pair(dest, k, v):
    return pl.pallas_call(
        pack_pair_body,
        in_specs=[whole(pltpu.SMEM), whole(pltpu.VMEM), whole(pltpu.VMEM)],
        out_specs=whole(pl.ANY),
        out_shape=jax.ShapeDtypeStruct((N_DP, KEY_HEADS, CAP, BR, 2 * HEAD), BF16),
        scratch_shapes=[
            pltpu.VMEM((SLOTS, KEY_HEADS, BR, 2 * HEAD), BF16),
            pltpu.SemaphoreType.DMA((SLOTS,)),
        ],
        name="pack_pair",
    )(dest, k, v)


def pack_wide_body(dest, q, g, out, sem):
    copies = []
    for j, (group, rank) in enumerate(route(dest)):
        for h in range(KEY_HEADS):
            for n, x in enumerate((q, g)):
                copies.append(pltpu.make_async_copy(
                    x.at[pl.ds(j * BR, BR), pl.ds(h * WIDE, WIDE)],
                    out.at[group, h, rank, :, pl.ds(n * WIDE, WIDE)],
                    sem.at[j, h, n]))
    run(copies)


def pack_wide(dest, q, g):
    return pl.pallas_call(
        pack_wide_body,
        in_specs=[whole(pltpu.SMEM), whole(pltpu.VMEM), whole(pltpu.VMEM)],
        out_specs=whole(pl.ANY),
        out_shape=jax.ShapeDtypeStruct((N_DP, KEY_HEADS, CAP, BR, 2 * WIDE), BF16),
        scratch_shapes=[pltpu.SemaphoreType.DMA((SLOTS, KEY_HEADS, 2))],
        name="pack_wide",
    )(dest, q, g)


def pick_body(t, x, out, sem):
    run([pltpu.make_async_copy(x.at[t[0, s], :, t[1, s]], out.at[s], sem.at[s])
         for s in range(SLOTS)])


def pick_pair(table, x):
    return pl.pallas_call(
        pick_body,
        in_specs=[whole(pltpu.SMEM), whole(pl.ANY)],
        out_specs=whole(pltpu.VMEM),
        out_shape=jax.ShapeDtypeStruct((SLOTS, N_Y, BR, 2 * HEAD), BF16),
        scratch_shapes=[pltpu.SemaphoreType.DMA((SLOTS,))],
        name="pick_pair",
    )(table, x)


def place_body(t, x, out, sem):
    run([pltpu.make_async_copy(x.at[s], out.at[t[0, s], :, t[1, s]], sem.at[s])
         for s in range(SLOTS)])


def place_pair(table, x):
    return pl.pallas_call(
        place_body,
        in_specs=[whole(pltpu.SMEM), whole(pltpu.VMEM)],
        out_specs=whole(pl.ANY),
        out_shape=jax.ShapeDtypeStruct((N_DP, N_Y, CAP, BR, 2 * HEAD), BF16),
        scratch_shapes=[pltpu.SemaphoreType.DMA((SLOTS,))],
        name="place_pair",
    )(table, x)


def home_wide_body(dest, x, out, sem):
    copies = []
    for j, (group, rank) in enumerate(route(dest)):
        for h in range(KEY_HEADS):
            copies.append(pltpu.make_async_copy(
                x.at[group, h, rank],
                out.at[pl.ds(j * BR, BR), pl.ds(h * WIDE, WIDE)],
                sem.at[j, h]))
    run(copies)


def home_wide(dest, x):
    return pl.pallas_call(
        home_wide_body,
        in_specs=[whole(pltpu.SMEM), whole(pl.ANY)],
        out_specs=whole(pltpu.VMEM),
        out_shape=jax.ShapeDtypeStruct((SLOTS * BR, QUERY_HEADS * HEAD), BF16),
        scratch_shapes=[pltpu.SemaphoreType.DMA((SLOTS, KEY_HEADS))],
        name="home_wide",
    )(dest, x)


def home_pair_body(dest, x, k, v, stage, sem):
    copies = []
    for j, (group, rank) in enumerate(route(dest)):
        copies.append(pltpu.make_async_copy(x.at[group, :, rank], stage.at[j], sem.at[j]))
    run(copies)
    for j in range(SLOTS):
        rows = slice(j * BR, (j + 1) * BR)
        for h in range(KEY_HEADS):
            cols = slice(h * HEAD, (h + 1) * HEAD)
            k[rows, cols] = stage[j, h, :, :HEAD]
            v[rows, cols] = stage[j, h, :, HEAD:]


def home_pair(dest, x):
    out = jax.ShapeDtypeStruct((SLOTS * BR, KEY_HEADS * HEAD), BF16)
    return pl.pallas_call(
        home_pair_body,
        in_specs=[whole(pltpu.SMEM), whole(pl.ANY)],
        out_specs=[whole(pltpu.VMEM), whole(pltpu.VMEM)],
        out_shape=[out, out],
        scratch_shapes=[
            pltpu.VMEM((SLOTS, KEY_HEADS, BR, 2 * HEAD), BF16),
            pltpu.SemaphoreType.DMA((SLOTS,)),
        ],
        name="home_pair",
    )(dest, x)


def dot_nt(a, b):
    return lax.dot_general(a, b, (((1,), (1,)), ((), ())), preferred_element_type=F32)


def dot_nn(a, b):
    return lax.dot_general(a, b, (((1,), (0,)), ((), ())), preferred_element_type=F32)


def fold_max(x):
    return jnp.max(x.reshape(x.shape[0] // 8, 8, x.shape[1]), axis=0)


def fold_sum(x):
    return jnp.sum(x.reshape(x.shape[0] // 8, 8, x.shape[1]), axis=0)


def attend_body(t, qg_ref, kv_ref, dq_ref, dkv_ref,
                ks, vs, kt, qm, gm, bias, sc, dp, acc_k, acc_v, dqt):
    s = pl.program_id(0)
    first = t[2, s]

    @pl.when(s == 0)
    def _():
        def lay(o, carry):
            for y in range(N_Y):
                rows = pl.ds(y * HEAD, HEAD)
                ks[o, rows] = kv_ref[:, o, y, :, :HEAD].reshape(HEAD, HEAD)
                vs[o, rows] = kv_ref[:, o, y, :, HEAD:].reshape(HEAD, HEAD)
            kt[o] = ks[o].T
            return carry

        lax.fori_loop(0, SLOTS, lay, 0)
        key = lax.broadcasted_iota(jnp.int32, (HALF, HALF), 0)
        lane = lax.broadcasted_iota(jnp.int32, (HALF, HALF), 1)
        query = (lane // HEAD) * HEAD + t[3, 0] * BR + lane % BR
        bias[...] = jnp.where(key <= query, 0.0, NEG).astype(F32)

    for y in range(N_Y):
        for h in range(PER_KEY):
            rows = pl.ds(y * HEAD + h * BR, BR)
            qm[rows, :] = qg_ref[0, y, 0, :, h * HEAD:(h + 1) * HEAD]
            gm[rows, :] = qg_ref[0, y, 0, :, WIDE + h * HEAD:WIDE + (h + 1) * HEAD]

    count = s - first
    own = SPAN - 1
    lo, hi = slice(0, HALF), slice(HALF, BLOCK)
    parts = ((lo, lo, True), (lo, hi, False), (hi, hi, True))

    top = {}
    for keys, rows, masked in parts:
        x = dot_nt(ks[s, keys], qm[rows])
        if masked:
            x = x + bias[...]
        sc[own, keys, rows] = x
        x = fold_max(x)
        top[rows.start] = jnp.maximum(top[rows.start], x) if rows.start in top else x
    top = jnp.concatenate([top[0], top[HALF]], axis=1)

    def score_step(i, top):
        x = dot_nt(ks[first + i], qm[...])
        sc[i] = x
        return jnp.maximum(top, fold_max(x))

    top = lax.fori_loop(0, count, score_step, top)
    top = jnp.max(top, axis=0, keepdims=True)

    total, moment = {}, {}
    for keys, rows, masked in parts:
        d = dot_nt(vs[s, keys], gm[rows])
        e = jnp.exp2((sc[own, keys, rows] - top[:, rows]) * EXP_SCALE)
        sc[own, keys, rows] = e
        dp[own, keys, rows] = d
        a, b = fold_sum(e), fold_sum(e * d)
        if rows.start in total:
            a, b = a + total[rows.start], b + moment[rows.start]
        total[rows.start], moment[rows.start] = a, b

    def exp_step(i, state):
        total, moment = state
        d = dot_nt(vs[first + i], gm[...])
        e = jnp.exp2((sc[i] - top) * EXP_SCALE)
        sc[i] = e
        dp[i] = d
        return total + fold_sum(e), moment + fold_sum(e * d)

    total, moment = lax.fori_loop(
        0, count, exp_step,
        (jnp.concatenate([total[0], total[HALF]], axis=1),
         jnp.concatenate([moment[0], moment[HALF]], axis=1)))
    inverse = 1.0 / jnp.sum(total, axis=0, keepdims=True)
    delta = jnp.sum(moment, axis=0, keepdims=True) * inverse

    for n, (keys, rows, masked) in enumerate(parts):
        p = sc[own, keys, rows] * inverse[:, rows]
        w = p.astype(BF16)
        ds = (p * (dp[own, keys, rows] - delta[:, rows])).astype(BF16)
        val_term = dot_nn(w, gm[rows])
        key_term = dot_nn(ds, qm[rows])
        qry_term = dot_nn(kt[s, :, keys], ds)
        if n == 1:
            acc_v[s, keys] += val_term
            acc_k[s, keys] += key_term
        else:
            acc_v[s, keys] = val_term
            acc_k[s, keys] = key_term
        if n == 2:
            dqt[:, rows] += qry_term
        else:
            dqt[:, rows] = qry_term

    def grad_step(i, carry):
        o = first + i
        p = sc[i] * inverse
        w = p.astype(BF16)
        ds = (p * (dp[i] - delta)).astype(BF16)
        acc_v[o] += dot_nn(w, gm[...])
        acc_k[o] += dot_nn(ds, qm[...])
        dqt[...] += dot_nn(kt[o], ds)
        return carry

    lax.fori_loop(0, count, grad_step, 0)

    dq = (dqt[...].T * SCALE).astype(BF16)
    for y in range(N_Y):
        for h in range(PER_KEY):
            at = y * HEAD + h * BR
            dq_ref[0, y, 0, :, h * HEAD:(h + 1) * HEAD] = dq[at:at + BR]

    @pl.when(s == SLOTS - 1)
    def _():
        def emit(o, carry):
            for y in range(N_Y):
                rows = pl.ds(y * HEAD, HEAD)
                dkv_ref[:, o, y, :, :HEAD] = (
                    (acc_k[o, rows] * SCALE).astype(BF16).reshape(N_Z, BR, HEAD))
                dkv_ref[:, o, y, :, HEAD:] = acc_v[o, rows].astype(BF16).reshape(N_Z, BR, HEAD)
            return carry

        lax.fori_loop(0, SLOTS, emit, 0)


def attend(table, qg, kv):
    both = pl.BlockSpec((1, N_Y, 1, BR, 2 * WIDE), to_source)
    wide = pl.BlockSpec((1, N_Y, 1, BR, WIDE), to_source)
    pair = pl.BlockSpec((N_Z, SLOTS, N_Y, BR, 2 * HEAD), lambda s, t: (0, 0, 0, 0, 0))
    return pl.pallas_call(
        attend_body,
        grid_spec=pltpu.PrefetchScalarGridSpec(
            num_scalar_prefetch=1,
            grid=(SLOTS,),
            in_specs=[both, pair],
            out_specs=[wide, pair],
            scratch_shapes=[
                pltpu.VMEM((SLOTS, BLOCK, HEAD), BF16),
                pltpu.VMEM((SLOTS, BLOCK, HEAD), BF16),
                pltpu.VMEM((SLOTS, HEAD, BLOCK), BF16),
                pltpu.VMEM((BLOCK, HEAD), BF16),
                pltpu.VMEM((BLOCK, HEAD), BF16),
                pltpu.VMEM((HALF, HALF), F32),
                pltpu.VMEM((SPAN, BLOCK, BLOCK), F32),
                pltpu.VMEM((SPAN, BLOCK, BLOCK), F32),
                pltpu.VMEM((SLOTS, BLOCK, HEAD), F32),
                pltpu.VMEM((SLOTS, BLOCK, HEAD), F32),
                pltpu.VMEM((HEAD, BLOCK), F32),
            ],
        ),
        out_shape=[
            jax.ShapeDtypeStruct((N_DP, N_Y, CAP, BR, WIDE), BF16),
            jax.ShapeDtypeStruct((N_Z, SLOTS, N_Y, BR, 2 * HEAD), BF16),
        ],
        compiler_params=params(48),
        name="attend",
    )(table, qg, kv)


def swap(x):
    flat = x.reshape((N_DP * N_Y,) + x.shape[2:])
    return lax.all_to_all(flat, ("dp", "y"), 0, 0, tiled=True).reshape(x.shape)


def shards(queries, keys, values, output_gradient, doc_lengths, dest_group, dest_slot):
    packed = pack_pair(dest_group, keys, values)
    doc_lengths, dest_slot, late, packed = lax.optimization_barrier(
        (doc_lengths, dest_slot, dest_group, packed))
    arrived = swap(packed)
    wide = pack_wide(late, queries, output_gradient)
    table = tables(doc_lengths, late, dest_slot)
    kv = lax.all_gather(pick_pair(table, arrived), "z", axis=0, tiled=False)
    dq, dkv = attend(table, swap(wide), kv)
    dkv = lax.psum_scatter(dkv, "z", scatter_dimension=0, tiled=False)
    grad_q = home_wide(dest_group, swap(dq))
    key_gradient, value_gradient = home_pair(dest_group, swap(place_pair(table, dkv)))
    return grad_q, key_gradient, value_gradient


def solution(mesh):
    grid = Mesh(mesh.devices.reshape(N_DP, N_Y, N_Z), ("dp", "y", "z"))
    rows = P(("dp", "y", "z"), None)
    return jax.shard_map(
        shards,
        mesh=grid,
        in_specs=(rows, rows, rows, rows, P(), P(), P()),
        out_specs=(rows, rows, rows),
        check_vma=False,
    )
```

```python
import math

import jax
import jax.numpy as jnp
from jax import lax
from jax.experimental import pallas as pl
from jax.experimental.pallas import tpu as pltpu
from jax.sharding import Mesh, PartitionSpec as P

QUERY_HEADS = 32
KEY_HEADS = 4
HEAD = 128
SLOTS = 8
BLOCK = 512
PER_KEY = QUERY_HEADS // KEY_HEADS
WIDE = PER_KEY * HEAD
SOON = 2 * HEAD
LATER = WIDE - SOON
BR = 16
CAP = 2
N_DP = 8
N_Y = 4
N_Z = 8
HALF = BLOCK // 2
CHUNK = (SLOTS, N_Y, BR, HEAD)
SPAN = SLOTS // 2
NEG = -1.0e30
TILE = 256
SCALE = HEAD ** -0.5
EXP_SCALE = SCALE / math.log(2.0)
F32 = jnp.float32
BF16 = jnp.bfloat16
MIB = 1024 * 1024


def tables(doc_lengths, dest_group, dest_slot):
    me = lax.axis_index("dp")
    blocks = jnp.arange(SLOTS, dtype=jnp.int32)
    dest = dest_group.reshape(N_DP, SLOTS)
    slot = dest_slot.reshape(N_DP, SLOTS)
    earlier = (dest[:, :, None] == dest[:, None, :]) & (blocks[None, :] < blocks[:, None])[None]
    rank = jnp.sum(earlier.astype(jnp.int32), axis=2)
    mine = blocks == me
    hit = ((dest == me)[None] & (slot[None] == blocks[:, None, None])).astype(jnp.int32)
    from_group = jnp.sum(hit * blocks[None, :, None], axis=(1, 2))
    from_rank = jnp.sum(hit * rank[None], axis=(1, 2))
    lengths = jnp.sum(jnp.where(mine[:, None], doc_lengths, 0), axis=0)
    docs = jnp.arange(lengths.shape[0], dtype=jnp.int32)
    ends = jnp.sum(jnp.where(docs[None, :] <= docs[:, None], lengths[None, :], 0), axis=1)
    first = jnp.max(jnp.where(ends[None, :] <= blocks[:, None], ends[None, :], 0), axis=1)
    place = jnp.full((SLOTS,), lax.axis_index("z"), jnp.int32)
    return jnp.stack([from_group, from_rank, first, place]).astype(jnp.int32)


def params(mib):
    return pltpu.CompilerParams(vmem_limit_bytes=mib * MIB)


def to_source(s, t):
    return (t[0, s], 0, t[1, s], 0, 0)


def whole(space):
    return pl.BlockSpec(memory_space=space)


def route(dest):
    base = lax.axis_index("dp") * SLOTS
    groups = [dest[base + j] for j in range(SLOTS)]
    ranks = []
    for j in range(SLOTS):
        rank = jnp.int32(0)
        for i in range(j):
            rank = rank + jnp.where(groups[i] == groups[j], 1, 0).astype(jnp.int32)
        ranks.append(rank)
    return list(zip(groups, ranks))


def run(copies):
    for copy in copies:
        copy.start()
    for copy in copies:
        copy.wait()


def pack_first_body(dest, k, v, q, g, out, part, stage, get, put):
    gets = [pltpu.make_async_copy(x.at[:, pl.ds(h * WIDE + LATER, SOON)], part.at[n, h],
                                  get.at[n, h])
            for n, x in enumerate((q, g)) for h in range(KEY_HEADS)]
    run(gets)
    puts = []
    for j, (group, rank) in enumerate(route(dest)):
        rows = slice(j * BR, (j + 1) * BR)
        for h in range(KEY_HEADS):
            cols = slice(h * HEAD, (h + 1) * HEAD)
            stage[j, h, :, :HEAD] = k[rows, cols]
            stage[j, h, :, HEAD:2 * HEAD] = v[rows, cols]
            stage[j, h, :, 2 * HEAD:2 * HEAD + SOON] = part[0, h, rows]
            stage[j, h, :, 2 * HEAD + SOON:] = part[1, h, rows]
        puts.append(pltpu.make_async_copy(stage.at[j], out.at[group, :, rank], put.at[j]))
        puts[-1].start()
    for copy in puts:
        copy.wait()


def pack_first(dest, k, v, q, g):
    width = 2 * HEAD + 2 * SOON
    return pl.pallas_call(
        pack_first_body,
        in_specs=[whole(pltpu.SMEM), whole(pltpu.VMEM), whole(pltpu.VMEM), whole(pl.ANY),
                  whole(pl.ANY)],
        out_specs=whole(pl.ANY),
        out_shape=jax.ShapeDtypeStruct((N_DP, KEY_HEADS, CAP, BR, width), BF16),
        scratch_shapes=[
            pltpu.VMEM((2, KEY_HEADS, SLOTS * BR, SOON), BF16),
            pltpu.VMEM((SLOTS, KEY_HEADS, BR, width), BF16),
            pltpu.SemaphoreType.DMA((2, KEY_HEADS)),
            pltpu.SemaphoreType.DMA((SLOTS,)),
        ],
        name="pack_first",
    )(dest, k, v, q, g)


def pack_rest_body(dest, q, g, out, sem):
    copies = []
    for j, (group, rank) in enumerate(route(dest)):
        for h in range(KEY_HEADS):
            for n, x in enumerate((q, g)):
                copies.append(pltpu.make_async_copy(
                    x.at[pl.ds(j * BR, BR), pl.ds(h * WIDE, LATER)],
                    out.at[group, h, rank, :, pl.ds(n * LATER, LATER)],
                    sem.at[j, h, n]))
    run(copies)


def pack_rest(dest, q, g):
    return pl.pallas_call(
        pack_rest_body,
        in_specs=[whole(pltpu.SMEM), whole(pltpu.VMEM), whole(pltpu.VMEM)],
        out_specs=whole(pl.ANY),
        out_shape=jax.ShapeDtypeStruct((N_DP, KEY_HEADS, CAP, BR, 2 * LATER), BF16),
        scratch_shapes=[pltpu.SemaphoreType.DMA((SLOTS, KEY_HEADS, 2))],
        name="pack_rest",
    )(dest, q, g)


def pick_body(t, x, k, v, stage, get, put):
    run([pltpu.make_async_copy(x.at[t[0, s], :, t[1, s], :, pl.ds(n * HEAD, HEAD)],
                               stage.at[n, s], get.at[n, s])
         for s in range(SLOTS) for n in range(2)])
    run([pltpu.make_async_copy(stage.at[n], out, put.at[n]) for n, out in enumerate((k, v))])


def pick_pair(table, x):
    out = jax.ShapeDtypeStruct(CHUNK, BF16)
    return pl.pallas_call(
        pick_body,
        in_specs=[whole(pltpu.SMEM), whole(pl.ANY)],
        out_specs=[whole(pltpu.HBM), whole(pltpu.HBM)],
        out_shape=[out, out],
        scratch_shapes=[
            pltpu.VMEM((2,) + CHUNK, BF16),
            pltpu.SemaphoreType.DMA((2, SLOTS)),
            pltpu.SemaphoreType.DMA((2,)),
        ],
        name="pick_pair",
    )(table, x)


def place_body(t, ka, kb, kc, va, vb, vc, out, stage, sem):
    copies = []
    for s in range(SLOTS):
        for n, (a, b, c) in enumerate(((ka, kb, kc), (va, vb, vc))):
            total = a[s].astype(F32) + b[s].astype(F32) + c[s].astype(F32)
            stage[s, :, :, n * HEAD:(n + 1) * HEAD] = total.astype(BF16)
        copies.append(pltpu.make_async_copy(stage.at[s], out.at[t[0, s], :, t[1, s]], sem.at[s]))
    run(copies)


def place_pair(table, dk, dv):
    return pl.pallas_call(
        place_body,
        in_specs=[whole(pltpu.SMEM)] + [whole(pltpu.VMEM)] * 6,
        out_specs=whole(pl.ANY),
        out_shape=jax.ShapeDtypeStruct((N_DP, N_Y, CAP, BR, 2 * HEAD), BF16),
        scratch_shapes=[
            pltpu.VMEM((SLOTS, N_Y, BR, 2 * HEAD), BF16),
            pltpu.SemaphoreType.DMA((SLOTS,)),
        ],
        name="place_pair",
    )(table, *dk, *dv)


def home_wide_body(dest, x, out, sem):
    copies = []
    for j, (group, rank) in enumerate(route(dest)):
        for h in range(KEY_HEADS):
            copies.append(pltpu.make_async_copy(
                x.at[group, h, rank],
                out.at[pl.ds(j * BR, BR), pl.ds(h * WIDE, WIDE)],
                sem.at[j, h]))
    run(copies)


def home_wide(dest, x):
    return pl.pallas_call(
        home_wide_body,
        in_specs=[whole(pltpu.SMEM), whole(pl.ANY)],
        out_specs=whole(pltpu.VMEM),
        out_shape=jax.ShapeDtypeStruct((SLOTS * BR, QUERY_HEADS * HEAD), BF16),
        scratch_shapes=[pltpu.SemaphoreType.DMA((SLOTS, KEY_HEADS))],
        name="home_wide",
    )(dest, x)


def home_pair_body(dest, x, k, v, stage, sem):
    copies = []
    for j, (group, rank) in enumerate(route(dest)):
        copies.append(pltpu.make_async_copy(x.at[group, :, rank], stage.at[j], sem.at[j]))
    run(copies)
    for j in range(SLOTS):
        rows = slice(j * BR, (j + 1) * BR)
        for h in range(KEY_HEADS):
            cols = slice(h * HEAD, (h + 1) * HEAD)
            k[rows, cols] = stage[j, h, :, :HEAD]
            v[rows, cols] = stage[j, h, :, HEAD:]


def home_pair(dest, x):
    out = jax.ShapeDtypeStruct((SLOTS * BR, KEY_HEADS * HEAD), BF16)
    return pl.pallas_call(
        home_pair_body,
        in_specs=[whole(pltpu.SMEM), whole(pl.ANY)],
        out_specs=[whole(pltpu.VMEM), whole(pltpu.VMEM)],
        out_shape=[out, out],
        scratch_shapes=[
            pltpu.VMEM((SLOTS, KEY_HEADS, BR, 2 * HEAD), BF16),
            pltpu.SemaphoreType.DMA((SLOTS,)),
        ],
        name="home_pair",
    )(dest, x)


def dot_nt(a, b):
    return lax.dot_general(a, b, (((1,), (1,)), ((), ())), preferred_element_type=F32)


def dot_nn(a, b):
    return lax.dot_general(a, b, (((1,), (0,)), ((), ())), preferred_element_type=F32)


def fold_max(x):
    return jnp.max(x.reshape(x.shape[0] // 8, 8, x.shape[1]), axis=0)


def fold_sum(x):
    return jnp.sum(x.reshape(x.shape[0] // 8, 8, x.shape[1]), axis=0)


def attend_body(t, soon_hbm, rest_hbm, *refs):
    ins, refs = refs[:2 * N_Z], refs[2 * N_Z:]
    dq_hbm, outs, refs = refs[0], refs[1:1 + 2 * N_Z], refs[1 + 2 * N_Z:]
    (soon_buf, rest_buf, kv_buf, dq_buf, dkv_buf, ks, vs, kt, qm, gm, bias, sc, dp, acc_k, acc_v,
     dqt, qg_in, kv_in, dq_out, dkv_out) = refs
    bands = (pl.ds(SPAN, SPAN), pl.ds(0, SPAN))
    z = t[3, 0]
    spots = [pl.multiple_of((z + r) % N_Z * BR, BR) for r in range(N_Z)]

    def qg_copies(s):
        return (
            pltpu.make_async_copy(
                soon_hbm.at[t[0, s], :, t[1, s], :, pl.ds(2 * HEAD, 2 * SOON)], soon_buf.at[s],
                qg_in.at[0, s]),
            pltpu.make_async_copy(
                rest_hbm.at[t[0, s], :, t[1, s]], rest_buf.at[s], qg_in.at[1, s]))

    def kv_copies(n):
        return [pltpu.make_async_copy(ins[i].at[bands[n]], kv_buf.at[i, bands[n]], kv_in.at[n, i])
                for i in range(2 * N_Z)]

    def dkv_copies(n):
        return [pltpu.make_async_copy(dkv_buf.at[i, bands[n]], outs[i].at[bands[n]],
                                      dkv_out.at[n, i])
                for i in range(2 * N_Z)]

    def dq_copy(s):
        return pltpu.make_async_copy(dq_buf.at[s], dq_hbm.at[t[0, s], :, t[1, s]], dq_out.at[s])

    for n in range(2):
        for copy in qg_copies(SLOTS - 1 - n * SPAN):
            copy.start()
        for copy in kv_copies(n):
            copy.start()
        for s in range(1, SPAN):
            for copy in qg_copies(SLOTS - 1 - n * SPAN - s):
                copy.start()

    key = lax.broadcasted_iota(jnp.int32, (HALF, HALF), 0)
    lane = lax.broadcasted_iota(jnp.int32, (HALF, HALF), 1)
    query = (lane // HEAD) * HEAD + t[3, 0] * BR + lane % BR
    bias[...] = jnp.where(key <= query, 0.0, NEG).astype(F32)
    halves = (slice(0, HALF), slice(HALF, BLOCK))
    own = SPAN - 1

    def lay(n, ready):
        o = ready - 1

        @pl.when(o == SPAN - 1)
        def _():
            for copy in kv_copies(1):
                copy.wait()

        for y in range(N_Y):
            for r in range(N_Z):
                rows = pl.ds(y * HEAD + spots[r], BR)
                ks[o, rows] = kv_buf[r, o, y]
                vs[o, rows] = kv_buf[N_Z + r, o, y]
        kt[o] = ks[o].T
        acc_k[o] = jnp.zeros((BLOCK, HEAD), F32)
        acc_v[o] = jnp.zeros((BLOCK, HEAD), F32)
        return o

    def step(n, ready):
        s = SLOTS - 1 - n
        first = t[2, s]
        ready = lax.fori_loop(0, ready - first, lay, ready)
        for copy in qg_copies(s):
            copy.wait()
        for y in range(N_Y):
            for h in range(PER_KEY):
                rows = pl.ds(y * HEAD + h * BR, BR)
                late = h * HEAD < LATER
                buf, span = (rest_buf, LATER) if late else (soon_buf, SOON)
                at = h * HEAD if late else h * HEAD - LATER
                qm[rows, :] = buf[s, y, :, at:at + HEAD]
                gm[rows, :] = buf[s, y, :, span + at:span + at + HEAD]
        count = s - first

        def score_tile(o, at, keys, rows, masked):
            top = None
            for k0 in range(keys.start, keys.stop, TILE):
                part = slice(k0, k0 + TILE)
                x = dot_nt(ks[o, part], qm[rows])
                if masked:
                    x = x + bias[k0 - keys.start:k0 - keys.start + TILE]
                sc[at, part, rows] = x
                x = fold_max(x)
                top = x if top is None else jnp.maximum(top, x)
            return top

        low, high = halves
        tops = (score_tile(s, own, low, low, True),
                jnp.maximum(score_tile(s, own, low, high, False),
                            score_tile(s, own, high, high, True)))

        def score_step(i, tops):
            full = slice(0, BLOCK)
            return tuple(jnp.maximum(top, score_tile(first + i, i, full, rows, False))
                         for top, rows in zip(tops, halves))

        tops = lax.fori_loop(0, count, score_step, tops)
        tops = [jnp.max(top, axis=0, keepdims=True) for top in tops]

        def exp_tile(o, at, keys, rows, top):
            total = moment = None
            for k0 in range(keys.start, keys.stop, TILE):
                part = slice(k0, k0 + TILE)
                d = dot_nt(vs[o, part], gm[rows])
                e = jnp.exp2((sc[at, part, rows] - top) * EXP_SCALE)
                sc[at, part, rows] = e
                dp[at, part, rows] = d
                a, b = fold_sum(e), fold_sum(e * d)
                total = a if total is None else total + a
                moment = b if moment is None else moment + b
            return total, moment

        def add(x, y):
            return tuple(a + b for a, b in zip(x, y))

        sums = (exp_tile(s, own, low, low, tops[0]),
                add(exp_tile(s, own, low, high, tops[1]), exp_tile(s, own, high, high, tops[1])))

        def exp_step(i, sums):
            full = slice(0, BLOCK)
            return tuple(add(old, exp_tile(first + i, i, full, rows, top))
                         for old, rows, top in zip(sums, halves, tops))

        sums = lax.fori_loop(0, count, exp_step, sums)
        inverse, delta = [], []
        for total, moment in sums:
            inverse.append(1.0 / jnp.sum(total, axis=0, keepdims=True))
            delta.append(jnp.sum(moment, axis=0, keepdims=True) * inverse[-1])
        inverse = jnp.concatenate(inverse, axis=1)
        delta = jnp.concatenate(delta, axis=1)

        def grad_tile(o, at, keys, rows, fresh):
            for k0 in range(keys.start, keys.stop, TILE):
                part = slice(k0, k0 + TILE)
                p = sc[at, part, rows] * inverse[:, rows]
                w = p.astype(BF16)
                ds = (p * (dp[at, part, rows] - delta[:, rows])).astype(BF16)
                acc_v[o, part] += dot_nn(w, gm[rows])
                acc_k[o, part] += dot_nn(ds, qm[rows])
                term = dot_nn(kt[o, :, part], ds)
                if fresh and k0 == keys.start:
                    dqt[:, rows] = term
                else:
                    dqt[:, rows] += term

        grad_tile(s, own, low, slice(0, BLOCK), True)
        grad_tile(s, own, high, high, False)

        def grad_step(i, carry):
            grad_tile(first + i, i, slice(0, BLOCK), slice(0, BLOCK), False)
            return carry

        lax.fori_loop(0, count, grad_step, 0)

        dq = (dqt[...] * SCALE).T.astype(BF16)
        for y in range(N_Y):
            for h in range(PER_KEY):
                at = y * HEAD + h * BR
                dq_buf[s, y, :, h * HEAD:(h + 1) * HEAD] = dq[at:at + BR]
            for r in range(N_Z):
                rows = pl.ds(y * HEAD + spots[r], BR)
                dkv_buf[r, s, y] = (acc_k[s, rows] * SCALE).astype(BF16)
                dkv_buf[N_Z + r, s, y] = acc_v[s, rows].astype(BF16)
        dq_copy(s).start()

        @pl.when(s == SPAN)
        def _():
            for copy in dkv_copies(0):
                copy.start()

        return ready

    for copy in kv_copies(0):
        copy.wait()
    lax.fori_loop(0, SLOTS, step, SLOTS)
    for copy in dkv_copies(1):
        copy.start()
    for n in range(2):
        for copy in dkv_copies(n):
            copy.wait()
    for s in reversed(range(SLOTS)):
        dq_copy(s).wait()


def attend(table, soon, rest, kv):
    out = pl.pallas_call(
        attend_body,
        in_specs=[whole(pltpu.SMEM), whole(pl.ANY), whole(pl.ANY)]
        + [whole(pltpu.HBM)] * (2 * N_Z),
        out_specs=[whole(pl.ANY)] + [whole(pltpu.HBM)] * (2 * N_Z),
        scratch_shapes=[
            pltpu.VMEM((SLOTS, N_Y, BR, 2 * SOON), BF16),
            pltpu.VMEM((SLOTS, N_Y, BR, 2 * LATER), BF16),
            pltpu.VMEM((2 * N_Z,) + CHUNK, BF16),
            pltpu.VMEM((SLOTS, N_Y, BR, WIDE), BF16),
            pltpu.VMEM((2 * N_Z,) + CHUNK, BF16),
            pltpu.VMEM((SLOTS, BLOCK, HEAD), BF16),
            pltpu.VMEM((SLOTS, BLOCK, HEAD), BF16),
            pltpu.VMEM((SLOTS, HEAD, BLOCK), BF16),
            pltpu.VMEM((BLOCK, HEAD), BF16),
            pltpu.VMEM((BLOCK, HEAD), BF16),
            pltpu.VMEM((HALF, HALF), F32),
            pltpu.VMEM((SPAN, BLOCK, BLOCK), F32),
            pltpu.VMEM((SPAN, BLOCK, BLOCK), F32),
            pltpu.VMEM((SLOTS, BLOCK, HEAD), F32),
            pltpu.VMEM((SLOTS, BLOCK, HEAD), F32),
            pltpu.VMEM((HEAD, BLOCK), F32),
            pltpu.SemaphoreType.DMA((2, SLOTS)),
            pltpu.SemaphoreType.DMA((2, 2 * N_Z)),
            pltpu.SemaphoreType.DMA((SLOTS,)),
            pltpu.SemaphoreType.DMA((2, 2 * N_Z)),
        ],
        out_shape=[jax.ShapeDtypeStruct((N_DP, N_Y, CAP, BR, WIDE), BF16)]
        + [jax.ShapeDtypeStruct(CHUNK, BF16)] * (2 * N_Z),
        compiler_params=params(63),
        name="attend",
    )(table, soon, rest, *kv)
    return out[0], out[1:1 + N_Z], out[1 + N_Z:]


def hop(x, step):
    return lax.ppermute(x, "z", [(i, (i + step) % N_Z) for i in range(N_Z)])


def spread(x):
    out = [x] * N_Z
    left = right = x
    for r in range(1, N_Z // 2 + 1):
        left = hop(left, -1)
        out[r] = left
        if r < N_Z // 2:
            right = hop(right, 1)
            out[N_Z - r] = right
    return out


def collect(chunks):
    half = N_Z // 2
    left, right = hop(chunks[half], -1), hop(chunks[half - 1], 1)
    for n in range(1, half):
        left = hop(plus(left, chunks[half + n]), -1)
        if n < half - 1:
            right = hop(plus(right, chunks[half - 1 - n]), 1)
    return left, right, chunks[0]


def plus(a, b):
    return (a.astype(F32) + b.astype(F32)).astype(BF16)


def swap(x):
    flat = x.reshape((N_DP * N_Y,) + x.shape[2:])
    return lax.all_to_all(flat, ("dp", "y"), 0, 0, tiled=True).reshape(x.shape)


def shards(queries, keys, values, output_gradient, doc_lengths, dest_group, dest_slot):
    packed = pack_first(dest_group, keys, values, queries, output_gradient)
    doc_lengths, dest_slot, late, packed = lax.optimization_barrier(
        (doc_lengths, dest_slot, dest_group, packed))
    arrived = swap(packed)
    rest = pack_rest(late, queries, output_gradient)
    table = tables(doc_lengths, late, dest_slot)
    k, v = pick_pair(table, arrived)
    dq, dk, dv = attend(table, arrived, swap(rest), spread(k) + spread(v))
    dq, pair = lax.optimization_barrier((swap(dq), place_pair(table, collect(dk), collect(dv))))
    grad_q = home_wide(dest_group, dq)
    key_gradient, value_gradient = home_pair(dest_group, swap(pair))
    return grad_q, key_gradient, value_gradient


def solution(mesh):
    grid = Mesh(mesh.devices.reshape(N_DP, N_Y, N_Z), ("dp", "y", "z"))
    rows = P(("dp", "y", "z"), None)
    return jax.shard_map(
        shards,
        mesh=grid,
        in_specs=(rows, rows, rows, rows, P(), P(), P()),
        out_specs=(rows, rows, rows),
        check_vma=False,
    )
```

```python
import functools
import math

import jax
import jax.numpy as jnp
from jax import lax
from jax.experimental import pallas as pl
from jax.experimental.pallas import tpu as pltpu
from jax.sharding import Mesh, PartitionSpec as P

QUERY_HEADS = 32
KEY_HEADS = 4
HEAD = 128
SLOTS = 8
BLOCK = 512
PER_KEY = QUERY_HEADS // KEY_HEADS
WIDE = PER_KEY * HEAD
SOON = 2 * HEAD
LATER = WIDE - SOON
BR = 16
CAP = 2
N_DP = 8
N_Y = 4
N_Z = 8
HALF = BLOCK // 2
CHUNK = (SLOTS, N_Y, BR, HEAD)
SPAN = SLOTS // 2
NEG = -1.0e30
TILE = 256
SCALE = HEAD ** -0.5
EXP_SCALE = SCALE / math.log(2.0)
F32 = jnp.float32
BF16 = jnp.bfloat16
MIB = 1024 * 1024


def tables(doc_lengths, dest_group, dest_slot):
    me = lax.axis_index("dp")
    blocks = jnp.arange(SLOTS, dtype=jnp.int32)
    dest = dest_group.reshape(N_DP, SLOTS)
    slot = dest_slot.reshape(N_DP, SLOTS)
    earlier = (dest[:, :, None] == dest[:, None, :]) & (blocks[None, :] < blocks[:, None])[None]
    rank = jnp.sum(earlier.astype(jnp.int32), axis=2)
    mine = blocks == me
    hit = ((dest == me)[None] & (slot[None] == blocks[:, None, None])).astype(jnp.int32)
    from_group = jnp.sum(hit * blocks[None, :, None], axis=(1, 2))
    from_rank = jnp.sum(hit * rank[None], axis=(1, 2))
    lengths = jnp.sum(jnp.where(mine[:, None], doc_lengths, 0), axis=0)
    docs = jnp.arange(lengths.shape[0], dtype=jnp.int32)
    ends = jnp.sum(jnp.where(docs[None, :] <= docs[:, None], lengths[None, :], 0), axis=1)
    first = jnp.max(jnp.where(ends[None, :] <= blocks[:, None], ends[None, :], 0), axis=1)
    place = jnp.full((SLOTS,), lax.axis_index("z"), jnp.int32)
    return jnp.stack([from_group, from_rank, first, place]).astype(jnp.int32)


def params(mib):
    return pltpu.CompilerParams(vmem_limit_bytes=mib * MIB)


def to_source(s, t):
    return (t[0, s], 0, t[1, s], 0, 0)


def whole(space):
    return pl.BlockSpec(memory_space=space)


def route(dest):
    base = lax.axis_index("dp") * SLOTS
    groups = [dest[base + j] for j in range(SLOTS)]
    ranks = []
    for j in range(SLOTS):
        rank = jnp.int32(0)
        for i in range(j):
            rank = rank + jnp.where(groups[i] == groups[j], 1, 0).astype(jnp.int32)
        ranks.append(rank)
    return list(zip(groups, ranks))


def run(copies):
    for copy in copies:
        copy.start()
    for copy in copies:
        copy.wait()


def pack_first_body(dest, k, v, q, g, out, part, stage, get, put):
    gets = [pltpu.make_async_copy(x.at[:, pl.ds(h * WIDE + LATER, SOON)], part.at[n, h],
                                  get.at[n, h])
            for n, x in enumerate((q, g)) for h in range(KEY_HEADS)]
    run(gets)
    puts = []
    for j, (group, rank) in enumerate(route(dest)):
        rows = slice(j * BR, (j + 1) * BR)
        for h in range(KEY_HEADS):
            cols = slice(h * HEAD, (h + 1) * HEAD)
            stage[j, h, :, :HEAD] = k[rows, cols]
            stage[j, h, :, HEAD:2 * HEAD] = v[rows, cols]
            stage[j, h, :, 2 * HEAD:2 * HEAD + SOON] = part[0, h, rows]
            stage[j, h, :, 2 * HEAD + SOON:] = part[1, h, rows]
        puts.append(pltpu.make_async_copy(stage.at[j], out.at[group, :, rank], put.at[j]))
        puts[-1].start()
    for copy in puts:
        copy.wait()


def pack_first(dest, k, v, q, g):
    width = 2 * HEAD + 2 * SOON
    return pl.pallas_call(
        pack_first_body,
        in_specs=[whole(pltpu.SMEM), whole(pltpu.VMEM), whole(pltpu.VMEM), whole(pl.ANY),
                  whole(pl.ANY)],
        out_specs=whole(pl.ANY),
        out_shape=jax.ShapeDtypeStruct((N_DP, KEY_HEADS, CAP, BR, width), BF16),
        scratch_shapes=[
            pltpu.VMEM((2, KEY_HEADS, SLOTS * BR, SOON), BF16),
            pltpu.VMEM((SLOTS, KEY_HEADS, BR, width), BF16),
            pltpu.SemaphoreType.DMA((2, KEY_HEADS)),
            pltpu.SemaphoreType.DMA((SLOTS,)),
        ],
        name="pack_first",
    )(dest, k, v, q, g)


def pack_rest_body(dest, q, g, out, sem):
    copies = []
    for j, (group, rank) in enumerate(route(dest)):
        for h in range(KEY_HEADS):
            for n, x in enumerate((q, g)):
                copies.append(pltpu.make_async_copy(
                    x.at[pl.ds(j * BR, BR), pl.ds(h * WIDE, LATER)],
                    out.at[group, h, rank, :, pl.ds(n * LATER, LATER)],
                    sem.at[j, h, n]))
    run(copies)


def pack_rest(dest, q, g):
    return pl.pallas_call(
        pack_rest_body,
        in_specs=[whole(pltpu.SMEM), whole(pltpu.VMEM), whole(pltpu.VMEM)],
        out_specs=whole(pl.ANY),
        out_shape=jax.ShapeDtypeStruct((N_DP, KEY_HEADS, CAP, BR, 2 * LATER), BF16),
        scratch_shapes=[pltpu.SemaphoreType.DMA((SLOTS, KEY_HEADS, 2))],
        name="pack_rest",
    )(dest, q, g)


def pick_body(t, x, k, v, soon, pair_stage, soon_stage, sem):
    for s in range(SLOTS):
        for y in range(N_Y):
            rows = x[t[0, s], y, t[1, s]]
            pair_stage[0, s, y] = rows[:, :HEAD]
            pair_stage[1, s, y] = rows[:, HEAD:2 * HEAD]
            soon_stage[s, y] = rows[:, 2 * HEAD:]
    run([pltpu.make_async_copy(pair_stage.at[0], k, sem.at[0]),
         pltpu.make_async_copy(pair_stage.at[1], v, sem.at[1]),
         pltpu.make_async_copy(soon_stage, soon, sem.at[2])])


def pick_first(table, x):
    out = jax.ShapeDtypeStruct(CHUNK, BF16)
    late = (SLOTS, N_Y, BR, 2 * SOON)
    return pl.pallas_call(
        pick_body,
        in_specs=[whole(pltpu.SMEM), whole(pltpu.VMEM)],
        out_specs=[whole(pltpu.HBM)] * 3,
        out_shape=[out, out, jax.ShapeDtypeStruct(late, BF16)],
        scratch_shapes=[
            pltpu.VMEM((2,) + CHUNK, BF16),
            pltpu.VMEM(late, BF16),
            pltpu.SemaphoreType.DMA((3,)),
        ],
        name="pick_first",
    )(table, x)


def place_body(t, ka, kb, kc, va, vb, vc, out):
    for s in range(SLOTS):
        for n, (a, b, c) in enumerate(((ka, kb, kc), (va, vb, vc))):
            total = a[s].astype(F32) + b[s].astype(F32) + c[s].astype(F32)
            out[t[0, s], :, t[1, s], :, n * HEAD:(n + 1) * HEAD] = total.astype(BF16)


def place_pair(table, dk, dv):
    return pl.pallas_call(
        place_body,
        in_specs=[whole(pltpu.SMEM)] + [whole(pltpu.VMEM)] * 6,
        out_specs=whole(pltpu.VMEM),
        out_shape=jax.ShapeDtypeStruct((N_DP, N_Y, CAP, BR, 2 * HEAD), BF16),
        name="place_pair",
    )(table, *dk, *dv)


def home_wide_body(dest, x, out, sem):
    copies = []
    for j, (group, rank) in enumerate(route(dest)):
        for h in range(KEY_HEADS):
            copies.append(pltpu.make_async_copy(
                x.at[group, h, rank],
                out.at[pl.ds(j * BR, BR), pl.ds(h * WIDE, WIDE)],
                sem.at[j, h]))
    run(copies)


def home_wide(dest, x):
    return pl.pallas_call(
        home_wide_body,
        in_specs=[whole(pltpu.SMEM), whole(pl.ANY)],
        out_specs=whole(pltpu.VMEM),
        out_shape=jax.ShapeDtypeStruct((SLOTS * BR, QUERY_HEADS * HEAD), BF16),
        scratch_shapes=[pltpu.SemaphoreType.DMA((SLOTS, KEY_HEADS))],
        name="home_wide",
    )(dest, x)


def home_pair_body(dest, x, k, v):
    for j, (group, rank) in enumerate(route(dest)):
        rows = slice(j * BR, (j + 1) * BR)
        for h in range(KEY_HEADS):
            cols = slice(h * HEAD, (h + 1) * HEAD)
            part = x[group, h, rank]
            k[rows, cols] = part[:, :HEAD]
            v[rows, cols] = part[:, HEAD:]


def home_pair(dest, x):
    out = jax.ShapeDtypeStruct((SLOTS * BR, KEY_HEADS * HEAD), BF16)
    return pl.pallas_call(
        home_pair_body,
        in_specs=[whole(pltpu.SMEM), whole(pltpu.VMEM)],
        out_specs=[whole(pltpu.VMEM), whole(pltpu.VMEM)],
        out_shape=[out, out],
        name="home_pair",
    )(dest, x)


def dot_nt(a, b):
    return lax.dot_general(a, b, (((1,), (1,)), ((), ())), preferred_element_type=F32)


def dot_nn(a, b):
    return lax.dot_general(a, b, (((1,), (0,)), ((), ())), preferred_element_type=F32)


def fold_max(x):
    return jnp.max(x.reshape(x.shape[0] // 8, 8, x.shape[1]), axis=0)


def fold_sum(x):
    return jnp.sum(x.reshape(x.shape[0] // 8, 8, x.shape[1]), axis=0)


def attend_body(t, soon_hbm, rest_hbm, *refs):
    ins, refs = refs[:2 * N_Z], refs[2 * N_Z:]
    dq_hbm, outs, refs = refs[0], refs[1:1 + 2 * N_Z], refs[1 + 2 * N_Z:]
    (soon_buf, rest_buf, kv_buf, dq_buf, dkv_buf, ks, vs, kt, qm, gm, bias, sc, dp, acc_k, acc_v,
     dqt, qg_in, kv_in, dq_out, dkv_out) = refs
    bands = (pl.ds(SPAN, SPAN), pl.ds(0, SPAN))
    z = t[3, 0]
    spots = [pl.multiple_of((z + r) % N_Z * BR, BR) for r in range(N_Z)]

    def qg_copies(s):
        return (
            pltpu.make_async_copy(
                soon_hbm.at[s], soon_buf.at[s], qg_in.at[0, s]),
            pltpu.make_async_copy(
                rest_hbm.at[t[0, s], :, t[1, s]], rest_buf.at[s], qg_in.at[1, s]))

    def kv_copies(n):
        return [pltpu.make_async_copy(ins[i].at[bands[n]], kv_buf.at[i, bands[n]], kv_in.at[n, i])
                for i in range(2 * N_Z)]

    def dkv_copies(n):
        return [pltpu.make_async_copy(dkv_buf.at[i, bands[n]], outs[i].at[bands[n]],
                                      dkv_out.at[n, i])
                for i in range(2 * N_Z)]

    def dq_copy(s):
        return pltpu.make_async_copy(dq_buf.at[s], dq_hbm.at[t[0, s], :, t[1, s]], dq_out.at[s])

    for n in range(2):
        for copy in qg_copies(SLOTS - 1 - n * SPAN):
            copy.start()
        for copy in kv_copies(n):
            copy.start()
        for s in range(1, SPAN):
            for copy in qg_copies(SLOTS - 1 - n * SPAN - s):
                copy.start()

    key = lax.broadcasted_iota(jnp.int32, (HALF, HALF), 0)
    lane = lax.broadcasted_iota(jnp.int32, (HALF, HALF), 1)
    query = (lane // HEAD) * HEAD + t[3, 0] * BR + lane % BR
    bias[...] = jnp.where(key <= query, 0.0, NEG).astype(F32)
    halves = (slice(0, HALF), slice(HALF, BLOCK))
    own = SPAN - 1

    def lay(n, ready):
        o = ready - 1

        @pl.when(o == SPAN - 1)
        def _():
            for copy in kv_copies(1):
                copy.wait()

        for y in range(N_Y):
            for r in range(N_Z):
                rows = pl.ds(y * HEAD + spots[r], BR)
                ks[o, rows] = kv_buf[r, o, y]
                vs[o, rows] = kv_buf[N_Z + r, o, y]
        kt[o] = ks[o].T
        acc_k[o] = jnp.zeros((BLOCK, HEAD), F32)
        acc_v[o] = jnp.zeros((BLOCK, HEAD), F32)
        return o

    def work(s, first, count):
        low, high = halves
        full = slice(0, BLOCK)
        blocks = [(first + i, i) for i in range(count)]

        def score_tile(o, at, keys, rows, masked):
            top = None
            for k0 in range(keys.start, keys.stop, TILE):
                part = slice(k0, k0 + TILE)
                x = dot_nt(ks[o, part], qm[rows])
                if masked:
                    x = x + bias[k0 - keys.start:k0 - keys.start + TILE]
                sc[at, part, rows] = x
                x = fold_max(x)
                top = x if top is None else jnp.maximum(top, x)
            return top

        tops = [score_tile(s, own, low, low, True),
                jnp.maximum(score_tile(s, own, low, high, False),
                            score_tile(s, own, high, high, True))]
        for o, i in blocks:
            tops = [jnp.maximum(top, score_tile(o, i, full, rows, False))
                    for top, rows in zip(tops, halves)]
        tops = [jnp.max(top, axis=0, keepdims=True) for top in tops]

        def exp_tile(o, at, keys, rows, top):
            total = moment = None
            for k0 in range(keys.start, keys.stop, TILE):
                part = slice(k0, k0 + TILE)
                d = dot_nt(vs[o, part], gm[rows])
                e = jnp.exp2((sc[at, part, rows] - top) * EXP_SCALE)
                sc[at, part, rows] = e
                dp[at, part, rows] = d
                a, b = fold_sum(e), fold_sum(e * d)
                total = a if total is None else total + a
                moment = b if moment is None else moment + b
            return total, moment

        def add(x, y):
            return tuple(a + b for a, b in zip(x, y))

        sums = [exp_tile(s, own, low, low, tops[0]),
                add(exp_tile(s, own, low, high, tops[1]), exp_tile(s, own, high, high, tops[1]))]
        for o, i in blocks:
            sums = [add(old, exp_tile(o, i, full, rows, top))
                    for old, rows, top in zip(sums, halves, tops)]
        inverse, delta = [], []
        for total, moment in sums:
            inverse.append(1.0 / jnp.sum(total, axis=0, keepdims=True))
            delta.append(jnp.sum(moment, axis=0, keepdims=True) * inverse[-1])
        inverse = jnp.concatenate(inverse, axis=1)
        delta = jnp.concatenate(delta, axis=1)

        def grad_tile(o, at, keys, rows, fresh):
            for k0 in range(keys.start, keys.stop, TILE):
                part = slice(k0, k0 + TILE)
                p = sc[at, part, rows] * inverse[:, rows]
                w = p.astype(BF16)
                ds = (p * (dp[at, part, rows] - delta[:, rows])).astype(BF16)
                acc_v[o, part] += dot_nn(w, gm[rows])
                acc_k[o, part] += dot_nn(ds, qm[rows])
                term = dot_nn(kt[o, :, part], ds)
                if fresh and k0 == keys.start:
                    dqt[:, rows] = term
                else:
                    dqt[:, rows] += term

        grad_tile(s, own, low, full, True)
        grad_tile(s, own, high, high, False)
        for y in range(N_Y):
            for r in range(N_Z):
                rows = pl.ds(y * HEAD + spots[r], BR)
                dkv_buf[r, s, y] = (acc_k[s, rows] * SCALE).astype(BF16)
                dkv_buf[N_Z + r, s, y] = acc_v[s, rows].astype(BF16)
        for o, i in blocks:
            grad_tile(o, i, full, full, False)
        dq = (dqt[...] * SCALE).T.astype(BF16)
        for y in range(N_Y):
            for h in range(PER_KEY):
                at = y * HEAD + h * BR
                dq_buf[s, y, :, h * HEAD:(h + 1) * HEAD] = dq[at:at + BR]

    def step(n, ready):
        s = SLOTS - 1 - n
        first = t[2, s]
        ready = lax.fori_loop(0, ready - first, lay, ready)
        for copy in qg_copies(s):
            copy.wait()
        for y in range(N_Y):
            for h in range(PER_KEY):
                rows = pl.ds(y * HEAD + h * BR, BR)
                late = h * HEAD < LATER
                buf, span = (rest_buf, LATER) if late else (soon_buf, SOON)
                at = h * HEAD if late else h * HEAD - LATER
                qm[rows, :] = buf[s, y, :, at:at + HEAD]
                gm[rows, :] = buf[s, y, :, span + at:span + at + HEAD]
        for count in range(SPAN):
            pl.when(s - first == count)(functools.partial(work, s, first, count))

        dq_copy(s).start()

        @pl.when(s == SPAN)
        def _():
            for copy in dkv_copies(0):
                copy.start()

        return ready

    for copy in kv_copies(0):
        copy.wait()
    lax.fori_loop(0, SLOTS, step, SLOTS)
    for copy in dkv_copies(1):
        copy.start()
    for n in range(2):
        for copy in dkv_copies(n):
            copy.wait()
    for s in reversed(range(SLOTS)):
        dq_copy(s).wait()


def attend(table, soon, rest, kv):
    out = pl.pallas_call(
        attend_body,
        in_specs=[whole(pltpu.SMEM), whole(pl.ANY), whole(pl.ANY)]
        + [whole(pltpu.HBM)] * (2 * N_Z),
        out_specs=[whole(pl.ANY)] + [whole(pltpu.HBM)] * (2 * N_Z),
        scratch_shapes=[
            pltpu.VMEM((SLOTS, N_Y, BR, 2 * SOON), BF16),
            pltpu.VMEM((SLOTS, N_Y, BR, 2 * LATER), BF16),
            pltpu.VMEM((2 * N_Z,) + CHUNK, BF16),
            pltpu.VMEM((SLOTS, N_Y, BR, WIDE), BF16),
            pltpu.VMEM((2 * N_Z,) + CHUNK, BF16),
            pltpu.VMEM((SLOTS, BLOCK, HEAD), BF16),
            pltpu.VMEM((SLOTS, BLOCK, HEAD), BF16),
            pltpu.VMEM((SLOTS, HEAD, BLOCK), BF16),
            pltpu.VMEM((BLOCK, HEAD), BF16),
            pltpu.VMEM((BLOCK, HEAD), BF16),
            pltpu.VMEM((HALF, HALF), F32),
            pltpu.VMEM((SPAN, BLOCK, BLOCK), F32),
            pltpu.VMEM((SPAN, BLOCK, BLOCK), F32),
            pltpu.VMEM((SLOTS, BLOCK, HEAD), F32),
            pltpu.VMEM((SLOTS, BLOCK, HEAD), F32),
            pltpu.VMEM((HEAD, BLOCK), F32),
            pltpu.SemaphoreType.DMA((2, SLOTS)),
            pltpu.SemaphoreType.DMA((2, 2 * N_Z)),
            pltpu.SemaphoreType.DMA((SLOTS,)),
            pltpu.SemaphoreType.DMA((2, 2 * N_Z)),
        ],
        out_shape=[jax.ShapeDtypeStruct((N_DP, N_Y, CAP, BR, WIDE), BF16)]
        + [jax.ShapeDtypeStruct(CHUNK, BF16)] * (2 * N_Z),
        compiler_params=params(63),
        name="attend",
    )(table, soon, rest, *kv)
    return out[0], out[1:1 + N_Z], out[1 + N_Z:]


def hop(x, step):
    return lax.ppermute(x, "z", [(i, (i + step) % N_Z) for i in range(N_Z)])


def spread(x):
    out = [x] * N_Z
    left = right = x
    for r in range(1, N_Z // 2 + 1):
        left = hop(left, -1)
        out[r] = left
        if r < N_Z // 2:
            right = hop(right, 1)
            out[N_Z - r] = right
    return out


def collect(chunks):
    half = N_Z // 2
    left, right = hop(chunks[half], -1), hop(chunks[half - 1], 1)
    for n in range(1, half):
        left = hop(plus(left, chunks[half + n]), -1)
        if n < half - 1:
            right = hop(plus(right, chunks[half - 1 - n]), 1)
    return left, right, chunks[0]


def plus(a, b):
    return (a.astype(F32) + b.astype(F32)).astype(BF16)


def swap(x):
    flat = x.reshape((N_DP * N_Y,) + x.shape[2:])
    return lax.all_to_all(flat, ("dp", "y"), 0, 0, tiled=True).reshape(x.shape)


def shards(queries, keys, values, output_gradient, doc_lengths, dest_group, dest_slot):
    packed = pack_first(dest_group, keys, values, queries, output_gradient)
    doc_lengths, dest_slot, late, packed = lax.optimization_barrier(
        (doc_lengths, dest_slot, dest_group, packed))
    arrived = swap(packed)
    rest = pack_rest(late, queries, output_gradient)
    table = tables(doc_lengths, late, dest_slot)
    k, v, soon = pick_first(table, arrived)
    dq, dk, dv = attend(table, soon, swap(rest), spread(k) + spread(v))
    dq, pair = lax.optimization_barrier((swap(dq), place_pair(table, collect(dk), collect(dv))))
    grad_q = home_wide(dest_group, dq)
    key_gradient, value_gradient = home_pair(dest_group, swap(pair))
    return grad_q, key_gradient, value_gradient


def solution(mesh):
    grid = Mesh(mesh.devices.reshape(N_DP, N_Y, N_Z), ("dp", "y", "z"))
    rows = P(("dp", "y", "z"), None)
    return jax.shard_map(
        shards,
        mesh=grid,
        in_specs=(rows, rows, rows, rows, P(), P(), P()),
        out_specs=(rows, rows, rows),
        check_vma=False,
    )
```

```python
import functools
import math

import jax
import jax.numpy as jnp
from jax import lax
from jax.experimental import pallas as pl
from jax.experimental.pallas import tpu as pltpu
from jax.sharding import Mesh, PartitionSpec as P

QUERY_HEADS = 32
KEY_HEADS = 4
HEAD = 128
SLOTS = 8
BLOCK = 512
PER_KEY = QUERY_HEADS // KEY_HEADS
WIDE = PER_KEY * HEAD
SOON = 2 * HEAD
LATER = WIDE - SOON
BR = 16
CAP = 2
N_DP = 8
N_Y = 4
N_Z = 8
HALF = BLOCK // 2
CHUNK = (SLOTS, N_Y, BR, HEAD)
SPAN = SLOTS // 2
NEG = -1.0e30
TILE = 256
SCALE = HEAD ** -0.5
EXP_SCALE = SCALE / math.log(2.0)
F32 = jnp.float32
BF16 = jnp.bfloat16
MIB = 1024 * 1024


def tables(doc_lengths, dest_group, dest_slot):
    me = lax.axis_index("dp")
    blocks = jnp.arange(SLOTS, dtype=jnp.int32)
    dest = dest_group.reshape(N_DP, SLOTS)
    slot = dest_slot.reshape(N_DP, SLOTS)
    earlier = (dest[:, :, None] == dest[:, None, :]) & (blocks[None, :] < blocks[:, None])[None]
    rank = jnp.sum(earlier.astype(jnp.int32), axis=2)
    mine = blocks == me
    hit = ((dest == me)[None] & (slot[None] == blocks[:, None, None])).astype(jnp.int32)
    from_group = jnp.sum(hit * blocks[None, :, None], axis=(1, 2))
    from_rank = jnp.sum(hit * rank[None], axis=(1, 2))
    lengths = jnp.sum(jnp.where(mine[:, None], doc_lengths, 0), axis=0)
    docs = jnp.arange(lengths.shape[0], dtype=jnp.int32)
    ends = jnp.sum(jnp.where(docs[None, :] <= docs[:, None], lengths[None, :], 0), axis=1)
    first = jnp.max(jnp.where(ends[None, :] <= blocks[:, None], ends[None, :], 0), axis=1)
    place = jnp.full((SLOTS,), lax.axis_index("z"), jnp.int32)
    return jnp.stack([from_group, from_rank, first, place]).astype(jnp.int32)


def params(mib):
    return pltpu.CompilerParams(vmem_limit_bytes=mib * MIB)


def to_source(s, t):
    return (t[0, s], 0, t[1, s], 0, 0)


def whole(space):
    return pl.BlockSpec(memory_space=space)


def route(dest):
    base = lax.axis_index("dp") * SLOTS
    groups = [dest[base + j] for j in range(SLOTS)]
    ranks = []
    for j in range(SLOTS):
        rank = jnp.int32(0)
        for i in range(j):
            rank = rank + jnp.where(groups[i] == groups[j], 1, 0).astype(jnp.int32)
        ranks.append(rank)
    return list(zip(groups, ranks))


def run(copies):
    for copy in copies:
        copy.start()
    for copy in copies:
        copy.wait()


def pack_first_body(dest, k, v, q, g, out, part, stage, get, put):
    gets = [pltpu.make_async_copy(x.at[:, pl.ds(h * WIDE + LATER, SOON)], part.at[n, h],
                                  get.at[n, h])
            for n, x in enumerate((q, g)) for h in range(KEY_HEADS)]
    run(gets)
    puts = []
    for j, (group, rank) in enumerate(route(dest)):
        rows = slice(j * BR, (j + 1) * BR)
        for h in range(KEY_HEADS):
            cols = slice(h * HEAD, (h + 1) * HEAD)
            stage[j, h, :, :HEAD] = k[rows, cols]
            stage[j, h, :, HEAD:2 * HEAD] = v[rows, cols]
            stage[j, h, :, 2 * HEAD:2 * HEAD + SOON] = part[0, h, rows]
            stage[j, h, :, 2 * HEAD + SOON:] = part[1, h, rows]
        puts.append(pltpu.make_async_copy(stage.at[j], out.at[group, :, rank], put.at[j]))
        puts[-1].start()
    for copy in puts:
        copy.wait()


def pack_first(dest, k, v, q, g):
    width = 2 * HEAD + 2 * SOON
    return pl.pallas_call(
        pack_first_body,
        in_specs=[whole(pltpu.SMEM), whole(pltpu.VMEM), whole(pltpu.VMEM), whole(pl.ANY),
                  whole(pl.ANY)],
        out_specs=whole(pl.ANY),
        out_shape=jax.ShapeDtypeStruct((N_DP, KEY_HEADS, CAP, BR, width), BF16),
        scratch_shapes=[
            pltpu.VMEM((2, KEY_HEADS, SLOTS * BR, SOON), BF16),
            pltpu.VMEM((SLOTS, KEY_HEADS, BR, width), BF16),
            pltpu.SemaphoreType.DMA((2, KEY_HEADS)),
            pltpu.SemaphoreType.DMA((SLOTS,)),
        ],
        name="pack_first",
    )(dest, k, v, q, g)


def pack_rest_body(dest, q, g, out, sem):
    copies = []
    for j, (group, rank) in enumerate(route(dest)):
        for h in range(KEY_HEADS):
            for n, x in enumerate((q, g)):
                copies.append(pltpu.make_async_copy(
                    x.at[pl.ds(j * BR, BR), pl.ds(h * WIDE, LATER)],
                    out.at[group, h, rank, :, pl.ds(n * LATER, LATER)],
                    sem.at[j, h, n]))
    run(copies)


def pack_rest(dest, q, g):
    return pl.pallas_call(
        pack_rest_body,
        in_specs=[whole(pltpu.SMEM), whole(pltpu.VMEM), whole(pltpu.VMEM)],
        out_specs=whole(pl.ANY),
        out_shape=jax.ShapeDtypeStruct((N_DP, KEY_HEADS, CAP, BR, 2 * LATER), BF16),
        scratch_shapes=[pltpu.SemaphoreType.DMA((SLOTS, KEY_HEADS, 2))],
        name="pack_rest",
    )(dest, q, g)


def pick_body(t, x, k, v, soon, pair_stage, soon_stage, sem):
    for s in range(SLOTS):
        for y in range(N_Y):
            rows = x[t[0, s], y, t[1, s]]
            pair_stage[0, s, y] = rows[:, :HEAD]
            pair_stage[1, s, y] = rows[:, HEAD:2 * HEAD]
            soon_stage[s, y] = rows[:, 2 * HEAD:]
    run([pltpu.make_async_copy(pair_stage.at[0], k, sem.at[0]),
         pltpu.make_async_copy(pair_stage.at[1], v, sem.at[1]),
         pltpu.make_async_copy(soon_stage, soon, sem.at[2])])


def pick_first(table, x):
    out = jax.ShapeDtypeStruct(CHUNK, BF16)
    late = (SLOTS, N_Y, BR, 2 * SOON)
    return pl.pallas_call(
        pick_body,
        in_specs=[whole(pltpu.SMEM), whole(pltpu.VMEM)],
        out_specs=[whole(pltpu.HBM)] * 3,
        out_shape=[out, out, jax.ShapeDtypeStruct(late, BF16)],
        scratch_shapes=[
            pltpu.VMEM((2,) + CHUNK, BF16),
            pltpu.VMEM(late, BF16),
            pltpu.SemaphoreType.DMA((3,)),
        ],
        compiler_params=params(8),
        name="pick_first",
    )(table, x)


def place_body(t, ka, kb, kc, va, vb, vc, out):
    for s in range(SLOTS):
        for n, (a, b, c) in enumerate(((ka, kb, kc), (va, vb, vc))):
            total = a[s].astype(F32) + b[s].astype(F32) + c[s].astype(F32)
            out[t[0, s], :, t[1, s], :, n * HEAD:(n + 1) * HEAD] = total.astype(BF16)


def place_pair(table, dk, dv):
    return pl.pallas_call(
        place_body,
        in_specs=[whole(pltpu.SMEM)] + [whole(pltpu.VMEM)] * 6,
        out_specs=whole(pltpu.VMEM),
        out_shape=jax.ShapeDtypeStruct((N_DP, N_Y, CAP, BR, 2 * HEAD), BF16),
        compiler_params=params(8),
        name="place_pair",
    )(table, *dk, *dv)


def home_wide_body(dest, x, out, sem):
    copies = []
    for j, (group, rank) in enumerate(route(dest)):
        for h in range(KEY_HEADS):
            copies.append(pltpu.make_async_copy(
                x.at[group, h, rank],
                out.at[pl.ds(j * BR, BR), pl.ds(h * WIDE, WIDE)],
                sem.at[j, h]))
    run(copies)


def home_wide(dest, x):
    return pl.pallas_call(
        home_wide_body,
        in_specs=[whole(pltpu.SMEM), whole(pl.ANY)],
        out_specs=whole(pltpu.VMEM),
        out_shape=jax.ShapeDtypeStruct((SLOTS * BR, QUERY_HEADS * HEAD), BF16),
        scratch_shapes=[pltpu.SemaphoreType.DMA((SLOTS, KEY_HEADS))],
        name="home_wide",
    )(dest, x)


def home_pair_body(dest, x, k, v):
    for j, (group, rank) in enumerate(route(dest)):
        rows = slice(j * BR, (j + 1) * BR)
        for h in range(KEY_HEADS):
            cols = slice(h * HEAD, (h + 1) * HEAD)
            part = x[group, h, rank]
            k[rows, cols] = part[:, :HEAD]
            v[rows, cols] = part[:, HEAD:]


def home_pair(dest, x):
    out = jax.ShapeDtypeStruct((SLOTS * BR, KEY_HEADS * HEAD), BF16)
    return pl.pallas_call(
        home_pair_body,
        in_specs=[whole(pltpu.SMEM), whole(pltpu.VMEM)],
        out_specs=[whole(pltpu.VMEM), whole(pltpu.VMEM)],
        out_shape=[out, out],
        compiler_params=params(8),
        name="home_pair",
    )(dest, x)


def dot_nt(a, b):
    return lax.dot_general(a, b, (((1,), (1,)), ((), ())), preferred_element_type=F32)


def dot_nn(a, b):
    return lax.dot_general(a, b, (((1,), (0,)), ((), ())), preferred_element_type=F32)


def fold_max(x):
    return jnp.max(x.reshape(x.shape[0] // 8, 8, x.shape[1]), axis=0)


def fold_sum(x):
    return jnp.sum(x.reshape(x.shape[0] // 8, 8, x.shape[1]), axis=0)


def attend_body(t, soon_hbm, rest_hbm, *refs):
    ins, refs = refs[:2 * N_Z], refs[2 * N_Z:]
    dq_hbm, outs, refs = refs[0], refs[1:1 + 2 * N_Z], refs[1 + 2 * N_Z:]
    (soon_buf, rest_buf, dq_buf, dkv_buf, ks, vs, kt, qm, gm, bias, sc, dp, acc_k, acc_v,
     dqt, qg_in, kv_in, dq_out, dkv_out) = refs
    bands = (pl.ds(SPAN, SPAN), pl.ds(0, SPAN))
    z = t[3, 0]
    spots = [pl.multiple_of((z + r) % N_Z * BR, BR) for r in range(N_Z)]

    def qg_copies(s):
        return (
            pltpu.make_async_copy(
                soon_hbm.at[s], soon_buf.at[s], qg_in.at[0, s]),
            pltpu.make_async_copy(
                rest_hbm.at[t[0, s], :, t[1, s]], rest_buf.at[s], qg_in.at[1, s]))

    def kv_copies(n):
        return [pltpu.make_async_copy(ins[c * N_Z + r].at[bands[n]],
                                      ref.at[bands[n], :, pl.ds(spots[r], BR), :],
                                      kv_in.at[n, c * N_Z + r])
                for c, ref in enumerate((ks, vs)) for r in range(N_Z)]

    def dkv_copies(n):
        return [pltpu.make_async_copy(dkv_buf.at[i, bands[n]], outs[i].at[bands[n]],
                                      dkv_out.at[n, i])
                for i in range(2 * N_Z)]

    def dq_copy(s):
        return pltpu.make_async_copy(dq_buf.at[s], dq_hbm.at[t[0, s], :, t[1, s]], dq_out.at[s])

    for n in range(2):
        for copy in qg_copies(SLOTS - 1 - n * SPAN):
            copy.start()
        for copy in kv_copies(n):
            copy.start()
        for s in range(1, SPAN):
            for copy in qg_copies(SLOTS - 1 - n * SPAN - s):
                copy.start()

    key = lax.broadcasted_iota(jnp.int32, (HALF, HALF), 0)
    lane = lax.broadcasted_iota(jnp.int32, (HALF, HALF), 1)
    query = (lane // HEAD) * HEAD + t[3, 0] * BR + lane % BR
    bias[...] = jnp.where(key <= query, 0.0, NEG).astype(F32)
    halves = (slice(0, HALF), slice(HALF, BLOCK))
    own = SPAN - 1
    acc_k[...] = jnp.zeros(acc_k.shape, F32)
    acc_v[...] = jnp.zeros(acc_v.shape, F32)

    def keys_of(ref, o, part):
        rows = ref[o, part.start // HEAD:part.stop // HEAD]
        return rows.reshape(part.stop - part.start, HEAD)

    def fill(s, at):
        for y in range(N_Y):
            for h in range(PER_KEY):
                rows = pl.ds(y * HEAD + h * BR, BR)
                late = h * HEAD < LATER
                buf, span = (rest_buf, LATER) if late else (soon_buf, SOON)
                col = h * HEAD if late else h * HEAD - LATER
                qm[at, rows, :] = buf[s, y, :, col:col + HEAD]
                gm[at, rows, :] = buf[s, y, :, span + col:span + col + HEAD]

    def finish(s, at):
        dq = (dqt[at] * SCALE).astype(BF16).T
        for y in range(N_Y):
            for h in range(PER_KEY):
                row = y * HEAD + h * BR
                dq_buf[s, y, :, h * HEAD:(h + 1) * HEAD] = dq[row:row + BR]


    def lay(n, ready):
        o = ready - 1

        @pl.when(o == SPAN - 1)
        def _():
            for copy in kv_copies(1):
                copy.wait()

        kt[o] = ks[o].reshape(BLOCK, HEAD).T
        return o

    def work(s, first, count):
        low, high = halves
        full = slice(0, BLOCK)
        blocks = [(first + i, i) for i in range(count)]
        now, other = lax.rem(s, 2), lax.rem(s + 1, 2)
        finish(s + 1, other)
        fill(jnp.maximum(s - 1, 0), other)

        def score_tile(o, at, keys, rows, masked):
            top = None
            for k0 in range(keys.start, keys.stop, TILE):
                part = slice(k0, k0 + TILE)
                x = dot_nt(keys_of(ks, o, part), qm[now, rows])
                if masked:
                    x = x + bias[k0 - keys.start:k0 - keys.start + TILE]
                sc[at, part, rows] = x
                x = fold_max(x)
                top = x if top is None else jnp.maximum(top, x)
            return top

        tops = [score_tile(s, own, low, low, True),
                jnp.maximum(score_tile(s, own, low, high, False),
                            score_tile(s, own, high, high, True))]
        for o, i in blocks:
            tops = [jnp.maximum(top, score_tile(o, i, full, rows, False))
                    for top, rows in zip(tops, halves)]
        tops = [jnp.max(top, axis=0, keepdims=True) for top in tops]

        def exp_tile(o, at, keys, rows, top):
            total = moment = None
            for k0 in range(keys.start, keys.stop, TILE):
                part = slice(k0, k0 + TILE)
                d = dot_nt(keys_of(vs, o, part), gm[now, rows])
                e = jnp.exp2((sc[at, part, rows] - top) * EXP_SCALE)
                sc[at, part, rows] = e
                dp[at, part, rows] = d
                a, b = fold_sum(e), fold_sum(e * d)
                total = a if total is None else total + a
                moment = b if moment is None else moment + b
            return total, moment

        def add(x, y):
            return tuple(a + b for a, b in zip(x, y))

        sums = [exp_tile(s, own, low, low, tops[0]),
                add(exp_tile(s, own, low, high, tops[1]), exp_tile(s, own, high, high, tops[1]))]
        for o, i in blocks:
            sums = [add(old, exp_tile(o, i, full, rows, top))
                    for old, rows, top in zip(sums, halves, tops)]
        inverse, delta = [], []
        for total, moment in sums:
            inverse.append(1.0 / jnp.sum(total, axis=0, keepdims=True))
            delta.append(jnp.sum(moment, axis=0, keepdims=True) * inverse[-1])
        inverse = jnp.concatenate(inverse, axis=1)
        delta = jnp.concatenate(delta, axis=1)

        def grad_tile(o, at, keys, rows, fresh):
            for k0 in range(keys.start, keys.stop, TILE):
                part = slice(k0, k0 + TILE)
                p = sc[at, part, rows] * inverse[:, rows]
                w = p.astype(BF16)
                ds = (p * (dp[at, part, rows] - delta[:, rows])).astype(BF16)
                acc_v[o, part] += dot_nn(w, gm[now, rows])
                acc_k[o, part] += dot_nn(ds, qm[now, rows])
                term = dot_nn(kt[o, :, part], ds)
                if fresh and k0 == keys.start:
                    dqt[now, :, rows] = term
                else:
                    dqt[now, :, rows] += term

        grad_tile(s, own, low, full, True)
        grad_tile(s, own, high, high, False)
        for y in range(N_Y):
            for r in range(N_Z):
                rows = pl.ds(y * HEAD + spots[r], BR)
                dkv_buf[r, s, y] = (acc_k[s, rows] * SCALE).astype(BF16)
                dkv_buf[N_Z + r, s, y] = acc_v[s, rows].astype(BF16)
        for o, i in blocks:
            grad_tile(o, i, full, full, False)

    def step(n, ready):
        s = SLOTS - 1 - n
        first = t[2, s]
        ready = lax.fori_loop(0, ready - first, lay, ready)

        @pl.when(s > 0)
        def _():
            for copy in qg_copies(s - 1):
                copy.wait()

        for count in range(SPAN):
            pl.when(s - first == count)(functools.partial(work, s, first, count))

        @pl.when(s < SLOTS - 1)
        def _():
            dq_copy(s + 1).start()

        @pl.when(s == SPAN)
        def _():
            for copy in dkv_copies(0):
                copy.start()

        return ready

    for copy in qg_copies(SLOTS - 1) + tuple(kv_copies(0)):
        copy.wait()
    fill(SLOTS - 1, (SLOTS - 1) % 2)
    lax.fori_loop(0, SLOTS, step, SLOTS)
    finish(0, 0)
    dq_copy(0).start()
    for copy in dkv_copies(1):
        copy.start()
    for n in range(2):
        for copy in dkv_copies(n):
            copy.wait()
    for s in reversed(range(SLOTS)):
        dq_copy(s).wait()


def attend(table, soon, rest, kv):
    out = pl.pallas_call(
        attend_body,
        in_specs=[whole(pltpu.SMEM), whole(pl.ANY), whole(pl.ANY)]
        + [whole(pltpu.HBM)] * (2 * N_Z),
        out_specs=[whole(pl.ANY)] + [whole(pltpu.HBM)] * (2 * N_Z),
        scratch_shapes=[
            pltpu.VMEM((SLOTS, N_Y, BR, 2 * SOON), BF16),
            pltpu.VMEM((SLOTS, N_Y, BR, 2 * LATER), BF16),
            pltpu.VMEM((SLOTS + 1, N_Y, BR, WIDE), BF16),
            pltpu.VMEM((2 * N_Z,) + CHUNK, BF16),
            pltpu.VMEM((SLOTS, N_Y, HEAD, HEAD), BF16),
            pltpu.VMEM((SLOTS, N_Y, HEAD, HEAD), BF16),
            pltpu.VMEM((SLOTS, HEAD, BLOCK), BF16),
            pltpu.VMEM((2, BLOCK, HEAD), BF16),
            pltpu.VMEM((2, BLOCK, HEAD), BF16),
            pltpu.VMEM((HALF, HALF), F32),
            pltpu.VMEM((SPAN, BLOCK, BLOCK), F32),
            pltpu.VMEM((SPAN, BLOCK, BLOCK), F32),
            pltpu.VMEM((SLOTS, BLOCK, HEAD), F32),
            pltpu.VMEM((SLOTS, BLOCK, HEAD), F32),
            pltpu.VMEM((2, HEAD, BLOCK), F32),
            pltpu.SemaphoreType.DMA((2, SLOTS)),
            pltpu.SemaphoreType.DMA((2, 2 * N_Z)),
            pltpu.SemaphoreType.DMA((SLOTS,)),
            pltpu.SemaphoreType.DMA((2, 2 * N_Z)),
        ],
        out_shape=[jax.ShapeDtypeStruct((N_DP, N_Y, CAP, BR, WIDE), BF16)]
        + [jax.ShapeDtypeStruct(CHUNK, BF16)] * (2 * N_Z),
        compiler_params=params(63),
        name="attend",
    )(table, soon, rest, *kv)
    return out[0], out[1:1 + N_Z], out[1 + N_Z:]


def hop(x, step):
    return lax.ppermute(x, "z", [(i, (i + step) % N_Z) for i in range(N_Z)])


def spread(x):
    out = [x] * N_Z
    left = right = x
    for r in range(1, N_Z // 2 + 1):
        left = hop(left, -1)
        out[r] = left
        if r < N_Z // 2:
            right = hop(right, 1)
            out[N_Z - r] = right
    return out


def collect(chunks):
    half = N_Z // 2
    left, right = hop(chunks[half], -1), hop(chunks[half - 1], 1)
    for n in range(1, half):
        left = hop(plus(left, chunks[half + n]), -1)
        if n < half - 1:
            right = hop(plus(right, chunks[half - 1 - n]), 1)
    return left, right, chunks[0]


def plus(a, b):
    return (a.astype(F32) + b.astype(F32)).astype(BF16)


def swap(x):
    flat = x.reshape((N_DP * N_Y,) + x.shape[2:])
    return lax.all_to_all(flat, ("dp", "y"), 0, 0, tiled=True).reshape(x.shape)


def shards(queries, keys, values, output_gradient, doc_lengths, dest_group, dest_slot):
    packed = pack_first(dest_group, keys, values, queries, output_gradient)
    doc_lengths, dest_slot, late, packed = lax.optimization_barrier(
        (doc_lengths, dest_slot, dest_group, packed))
    arrived = swap(packed)
    rest = pack_rest(late, queries, output_gradient)
    table = tables(doc_lengths, late, dest_slot)
    k, v, soon = pick_first(table, arrived)
    dq, dk, dv = attend(table, soon, swap(rest), spread(k) + spread(v))
    dq, pair = lax.optimization_barrier((swap(dq), place_pair(table, collect(dk), collect(dv))))
    grad_q = home_wide(dest_group, dq)
    key_gradient, value_gradient = home_pair(dest_group, swap(pair))
    return grad_q, key_gradient, value_gradient


def solution(mesh):
    grid = Mesh(mesh.devices.reshape(N_DP, N_Y, N_Z), ("dp", "y", "z"))
    rows = P(("dp", "y", "z"), None)
    return jax.shard_map(
        shards,
        mesh=grid,
        in_specs=(rows, rows, rows, rows, P(), P(), P()),
        out_specs=(rows, rows, rows),
        check_vma=False,
    )
```
